128 devices in a mesh: group: 8 (over z, core), seq: 16 (over x, y).
Axes of the slice: x: 4, y: 4, z: 4, core: 2. Of those that a mesh axis runs over, the one named last changes fastest.
Arguments:
- queries: bfloat16 [8, 64, 8192], P('group', 'seq'), may hold values from -40 to 40
- prefix_keys: bfloat16 [8, 4, 4, 32768, 128], P('group', None, None, 'seq'), may hold values from -8 to 8
- prefix_values: bfloat16 [8, 4, 4, 32768, 128], P('group', None, None, 'seq'), may hold values from -48 to 48
- cont_keys: bfloat16 [8, 64, 4, 512, 128], P('group', 'seq'), may hold values from -11 to 11
- cont_values: bfloat16 [8, 64, 4, 512, 128], P('group', 'seq'), may hold values from -48 to 48
- cont_len: int32 [8, 64], P('group', 'seq'), may hold values from 1 to 512, as said below
- prompt_of: int32 [8, 64], P('group'), may hold values from 0 to 3, as said below
- w_out: bfloat16 [8192, 4096], P(None, 'group'), may hold values from -0.0625 to 0.0625
Outputs:
- projected: bfloat16 [8, 64, 4096], P('group', 'seq')
The draws below stay inside these ranges and needn't reach their ends.
Inputs may be any that keep to these rules, and one draw needn't show every extreme that they name: `prompt_of`: within a group each of the 4 prompts is continued by exactly 16 samples. `cont_len`: in every group some sample has 512 live positions.
All inputs are finite; a program needn't handle non-finite values.
Results may differ from the reference program's by a relative error of at most 0.02.
Values may be sent and summed in bfloat16 or wider, within the bound.
No kernel may reach another device: no remote copies, remote signals or barrier semaphores. Data moves between devices by JAX's collectives and lax.ppermute only.
A program may use at most 192 MiB of HBM per device.

```python
import jax
import jax.numpy as jnp
from jax import lax

HEADS = 64
KVH = 4
HD = 128
D = 4096
SAMP_PROMPT = 16
CONT_MAX = 512
SAMPLES = 64
PROMPTS = 4
PREFIX = 32768
N_GROUP = 8


def shared_layout(key):
    group_keys = jax.random.split(jax.random.fold_in(key, 101), N_GROUP)

    def shuffled(group_key):
        return jax.random.permutation(group_key, SAMPLES)
    ranks = jax.vmap(shuffled)(group_keys)
    prompt_ids = (ranks // SAMP_PROMPT).astype(jnp.int32)
    quiet_head = jax.random.randint(jax.random.fold_in(key, 104), (N_GROUP,), 0, KVH)
    damping = jnp.where(jnp.arange(KVH)[None, :] == quiet_head[:, None], 0.12, 1.0).astype(jnp.float32)
    return (prompt_ids, damping)


def draw_prompt_of(key, part):
    prompt_ids, damping = shared_layout(key)
    return prompt_ids


def draw_prefix_keys(key, part):
    prompt_ids, damping = shared_layout(key)
    key = jax.random.fold_in(key, 11)
    shape_all = (N_GROUP, PROMPTS, KVH, PREFIX, HD)
    result = jax.random.truncated_normal(key, -6.0, 6.0, shape_all, jnp.float32)
    result = result * damping[:, None, :, None, None]
    return result.astype(jnp.bfloat16)


def draw_cont_keys(key, part):
    prompt_ids, damping = shared_layout(key)
    key = jax.random.fold_in(key, 17)
    shape_all = (N_GROUP, SAMPLES, KVH, CONT_MAX, HD)
    result = 1.7 * jax.random.truncated_normal(key, -6.0, 6.0, shape_all, jnp.float32)
    result = result * damping[:, None, :, None, None]
    return result.astype(jnp.bfloat16)


def draw_queries(key, part):
    prompt_ids, damping = shared_layout(key)
    key = jax.random.fold_in(key, 13)
    shape_q = (N_GROUP, SAMPLES, KVH, HEADS // KVH, HD)
    quieted = (damping < 0.5)[:, None, :, None, None]
    drawn = 2.0 * jax.random.truncated_normal(key, -6.0, 6.0, shape_q, jnp.float32)
    strong = 16.0 * jax.random.truncated_normal(jax.random.fold_in(key, 3), -2.45, 2.45, shape_q, jnp.float32)
    result = jnp.where(quieted, strong, drawn)
    return result.reshape(N_GROUP, SAMPLES, HEADS * HD).astype(jnp.bfloat16)


def draw_cont_len(key, part):
    key = jax.random.fold_in(key, 7)
    first_key, second_key, third_key = jax.random.split(key, 3)
    first = jax.random.randint(first_key, (N_GROUP, SAMPLES), 1, CONT_MAX + 1)
    second = jax.random.randint(second_key, (N_GROUP, SAMPLES), 1, CONT_MAX + 1)
    lengths = jnp.maximum(1, first * second // CONT_MAX)
    picked = jax.random.randint(third_key, (N_GROUP, 1), 0, SAMPLES)
    lengths = jnp.where(jnp.arange(SAMPLES)[None, :] == picked, CONT_MAX, lengths)
    return lengths.astype(jnp.int32)


def level_of(own_key, shape, cuts, smallest, largest):
    def one(dim, parts):
        draws = jax.random.uniform(jax.random.fold_in(jax.random.fold_in(own_key, 6), dim), (parts,), jnp.float32, smallest / len(cuts), largest / len(cuts))
        return jnp.repeat(jnp.exp(draws), shape[dim] // parts).reshape((-1,) + (1,) * (len(shape) - dim - 1))

    factor_of = one(*cuts[0])
    for cut in cuts[1:]:
        factor_of = factor_of * one(*cut)
    return factor_of


def centred(key, extent, deviation, most, cuts=(), dtype=jnp.bfloat16):
    gain = level_of(key, extent, cuts, -0.22, 0.18) if cuts else 1.0
    entries = jax.random.normal(key, extent, jnp.float32) * deviation * gain
    return jnp.minimum(jnp.maximum(entries, -most), most).astype(dtype)


def setup_inputs(seed: int = 0) -> dict:
    keys = jax.random.split(jax.random.key(seed), 9)
    queries = draw_queries(jax.random.fold_in(keys[8], 71), 0)
    prefix_keys = draw_prefix_keys(jax.random.fold_in(keys[8], 71), 0)
    prefix_values = centred(keys[2], (N_GROUP, PROMPTS, KVH, PREFIX, HD), 8.0, 48.0, ((0, 8), (3, 16)))
    cont_keys = draw_cont_keys(jax.random.fold_in(keys[8], 71), 0)
    cont_values = centred(keys[4], (N_GROUP, SAMPLES, KVH, CONT_MAX, HD), 8.0, 48.0, ((0, 8), (1, 16)))
    cont_len = draw_cont_len(jax.random.fold_in(keys[8], 71), 0)
    prompt_of = draw_prompt_of(jax.random.fold_in(keys[8], 71), 0)
    w_out = centred(keys[7], (HEADS * HD, D), (HEADS * HD) ** -0.5, 0.0625, ((1, 8),))
    return {"queries": queries, "prefix_keys": prefix_keys, "prefix_values": prefix_values, "cont_keys": cont_keys, "cont_values": cont_values, "cont_len": cont_len, "prompt_of": prompt_of, "w_out": w_out}


def reference(queries, prefix_keys, prefix_values, cont_keys, cont_values, cont_len, prompt_of, w_out):
    scaling = HD ** -0.5
    per_group = HEADS // KVH

    def one_group(bundle):
        query_now, keys_now, values_now, ckeys_now, cvalues_now, lengths, prompt_ids = bundle
        sorting = jnp.argsort(prompt_ids, stable=True).astype(jnp.int32)
        inverse = jnp.argsort(sorting, stable=True).astype(jnp.int32)
        query_sorted = query_now[sorting].astype(jnp.float32).reshape(PROMPTS, SAMP_PROMPT, KVH, per_group, HD)
        ckeys_sorted = ckeys_now[sorting].reshape(PROMPTS, SAMP_PROMPT, KVH, CONT_MAX, HD)
        cvalues_sorted = cvalues_now[sorting].reshape(PROMPTS, SAMP_PROMPT, KVH, CONT_MAX, HD)
        lengths_sorted = lengths[sorting].reshape(PROMPTS, SAMP_PROMPT)

        def one_prompt(inner):
            query_p, keys_p, values_p, ckeys_p, cvalues_p, lengths_p = inner
            logits_pre = jnp.einsum('skjd,ktd->skjt', query_p, keys_p.astype(jnp.float32)) * scaling
            logits_new = jnp.einsum('skjd,sktd->skjt', query_p, ckeys_p.astype(jnp.float32)) * scaling
            usable = jnp.arange(CONT_MAX)[None, None, None, :] < lengths_p[:, None, None, None]
            logits_new = jnp.where(usable, logits_new, -jnp.inf)
            highest = jnp.maximum(logits_pre.max(-1), logits_new.max(-1))
            weights_pre = jnp.exp(logits_pre - highest[..., None])
            weights_new = jnp.exp(logits_new - highest[..., None])
            totals = weights_pre.sum(-1) + weights_new.sum(-1)
            rounded_pre = weights_pre.astype(jnp.bfloat16).astype(jnp.float32)
            rounded_new = weights_new.astype(jnp.bfloat16).astype(jnp.float32)
            summed = jnp.einsum('skjt,ktd->skjd', rounded_pre, values_p.astype(jnp.float32))
            summed = summed + jnp.einsum('skjt,sktd->skjd', rounded_new, cvalues_p.astype(jnp.float32))
            return summed / totals[..., None]

        mixed = lax.map(one_prompt, (query_sorted, keys_now, values_now, ckeys_sorted, cvalues_sorted, lengths_sorted))
        mixed = mixed.reshape(SAMPLES, HEADS * HD)[inverse].astype(jnp.bfloat16)
        return jnp.dot(mixed, w_out, preferred_element_type=jnp.float32).astype(jnp.bfloat16)

    return lax.map(one_group, (queries, prefix_keys, prefix_values, cont_keys, cont_values, cont_len, prompt_of))
```

```python
import functools

import jax
import jax.numpy as jnp
import numpy as np
from jax import lax
from jax.experimental import pallas as pl
from jax.experimental.pallas import tpu as pltpu
from jax.sharding import PartitionSpec as P

HEADS = 64
KVH = 4
HD = 128
PER = HEADS // KVH
PROMPTS = 4
SAMP = 16
CHUNKS = 2
KC = KVH // CHUNKS
HC = HEADS // CHUNKS
T_LOCAL = 2048
CONT = 512
D = 4096
LOG2E = float(np.log2(np.e))
SCALE2 = float(np.log2(np.e) / np.sqrt(HD))
BF = jnp.bfloat16
F32 = jnp.float32
VMEM = pl.BlockSpec(memory_space=pltpu.VMEM)
SMEM = pl.BlockSpec(memory_space=pltpu.SMEM)
ANY = pl.BlockSpec(memory_space=pl.ANY)

SWAP = np.zeros((256, 256), np.float32)
for _j in range(16):
    for _i in range(16):
        SWAP[16 * _j + _i, 16 * _i + _j] = 1


def dot(a, b):
    return jnp.dot(a, b, preferred_element_type=F32)


def dot_t(a, b):
    return lax.dot_general(a, b, (((1,), (1,)), ((), ())), preferred_element_type=F32)


def split3(x):
    hi = x.astype(BF).astype(F32)
    mid = (x - hi).astype(BF).astype(F32)
    return hi, mid, x - hi - mid


def iota(shape, dim):
    return lax.broadcasted_iota(jnp.int32, shape, dim)


def cont_kernel(len_ref, q_ref, k_hbm, v_hbm, tail_ref, kb, vb, sem):
    def copies(s):
        return (
            pltpu.make_async_copy(k_hbm.at[s], kb.at[s], sem.at[s, 0]),
            pltpu.make_async_copy(v_hbm.at[s], vb.at[s], sem.at[s, 1]),
        )

    for s in range(4):
        for c in copies(s):
            c.start()
    tail_ref[...] = jnp.zeros_like(tail_ref)
    lane = iota((16, 128), 1)
    row = iota((16, 128), 0)
    logs = [jnp.zeros((8, 128), F32) for _ in range(KVH)]
    for s in range(4):
        for c in copies(s):
            c.wait()
        live = iota((16, CONT), 1) < len_ref[s]
        for k in range(KVH):
            logit = jnp.where(live, dot_t(q_ref[s, 16 * k : 16 * k + 16], kb[s, k]), -jnp.inf)
            top = logit.max(1, keepdims=True)
            w = jnp.exp2((logit - top) * SCALE2)
            total = w.sum(1, keepdims=True)
            o = dot(w.astype(BF), vb[s, k]) * (1.0 / total)
            lse = top * SCALE2 + jnp.log(total) * LOG2E
            c, kk = k // KC, k % KC
            for j in range(16):
                tail_ref[c, 8 * kk + j // 2, (j % 2) * 4 + s : (j % 2) * 4 + s + 1, :] = o[j : j + 1]
            spread = jnp.where(lane == (row % 2) * 4 + s, jnp.broadcast_to(lse, (16, 128)), 0.0)
            logs[k] = logs[k] + spread.reshape(8, 2, 128).sum(1)
    for k in range(KVH):
        c, kk = k // KC, k % KC
        for n, part in enumerate(split3(logs[k])):
            for d in range(8):
                tail_ref[c, 8 * kk + d, 11 + n : 12 + n, :] = part[d : d + 1]


def cont_call(lengths, q, keys, values):
    return pl.pallas_call(
        cont_kernel,
        out_shape=jax.ShapeDtypeStruct((CHUNKS, 16, 16, 128), F32),
        in_specs=[SMEM, VMEM, ANY, ANY],
        out_specs=VMEM,
        scratch_shapes=[
            pltpu.VMEM((4, KVH, CONT, HD), BF),
            pltpu.VMEM((4, KVH, CONT, HD), BF),
            pltpu.SemaphoreType.DMA((4, 2)),
        ],
        compiler_params=pltpu.CompilerParams(vmem_limit_bytes=60 * 2**20),
        cost_estimate=pl.CostEstimate(flops=2 * 10**8, bytes_accessed=2**22, transcendentals=131072),
        name="cont",
    )(lengths, q, keys, values)


NB = KC * PROMPTS
TC = 512


def prefix_kernel(chunk, order, q_hbm, swap_ref, tail_ref, k_hbm, v_hbm, o_ref, qv, qs, kb, vb, sbuf, st, qsem, ks, vs):
    cq = pltpu.make_async_copy(q_hbm.at[:, KC * chunk : KC * chunk + KC], qv, qsem)
    cq.start()

    def copies(b):
        kq, p = b // PROMPTS, b % PROMPTS
        return (
            pltpu.make_async_copy(k_hbm.at[p, KC * chunk + kq], kb.at[b], ks.at[b]),
            pltpu.make_async_copy(v_hbm.at[p, KC * chunk + kq], vb.at[b], vs.at[b]),
        )

    for b in range(NB):
        for c in copies(b):
            c.start()
    cq.wait()
    for b in range(NB):
        kq, p = b // PROMPTS, b % PROMPTS
        for i in range(SAMP):
            qs[b, 16 * i : 16 * i + 16] = qv[order[16 * p + i], kq]
        qs[b] = dot(swap_ref[...], qs[b]).astype(BF)

    row = iota((256, 128), 0) % 32
    lane = iota((256, 128), 1)

    def finish(b, o, top, total):
        kq, p = b // PROMPTS, b % PROMPTS
        o = (o * (1.0 / total)).astype(BF)
        o_ref[8 * kq : 8 * kq + 8, 32 * p : 32 * p + 32, :] = o.reshape(8, 32, 128)
        lse = top * SCALE2 + jnp.log(total) * LOG2E
        spread = jnp.where(lane == p * 32 + row, jnp.broadcast_to(lse, (256, 128)), 0.0)
        spread = spread.reshape(8, 32, 128).sum(1)
        if p == 0:
            st[kq] = spread
        else:
            st[kq] = st[kq] + spread

    prev_top = None
    for b in range(NB + 1):
        peak = None
        if b < NB:
            for c in copies(b):
                c.wait()
            q = qs[b]
        if b > 0:
            acc = total = None
        for t in range(T_LOCAL // TC):
            cols = slice(t * TC, (t + 1) * TC)
            if b < NB:
                s = dot_t(q, kb[b, cols])
                sbuf[b % 2, :, cols] = s
                for z in range(TC // 128):
                    piece = s[:, 128 * z : 128 * z + 128]
                    peak = piece if peak is None else jnp.maximum(peak, piece)
            if b > 0:
                w = jnp.exp2((sbuf[(b - 1) % 2, :, cols] - prev_top) * SCALE2)
                for z in range(TC // 128):
                    piece = w[:, 128 * z : 128 * z + 128]
                    total = piece if total is None else total + piece
                o = dot(w.astype(BF), vb[b - 1, cols])
                acc = o if acc is None else acc + o
        if b > 0:
            finish(b - 1, acc, prev_top, total.sum(1, keepdims=True))
        if b < NB:
            prev_top = peak.max(1, keepdims=True)
    for kq in range(KC):
        parts = split3(st[kq])
        for d in range(8):
            dest = 8 * kq + d
            tail_ref[0, dest, 8:9, :] = parts[0][d : d + 1]
            tail_ref[0, dest, 9:10, :] = parts[1][d : d + 1]
            tail_ref[0, dest, 10:11, :] = parts[2][d : d + 1]
    o_ref[:, 128:144, :] = tail_ref[0].astype(BF)


def prefix_body(chunk, order, q_hbm, swap_ref, tail_in, k_hbm, v_hbm, o_ref, tail, *rest):
    tail[...] = tail_in[chunk : chunk + 1]
    prefix_kernel(chunk, order, q_hbm, swap_ref, tail, k_hbm, v_hbm, o_ref, *rest)


def prefix_call(chunk, order, q, swap, tail, keys, values):
    return pl.pallas_call(
        functools.partial(prefix_body, chunk),
        out_shape=jax.ShapeDtypeStruct((16, 144, 128), BF),
        in_specs=[SMEM, ANY, VMEM, VMEM, ANY, ANY],
        out_specs=VMEM,
        scratch_shapes=[
            pltpu.VMEM((1, 16, 16, 128), F32),
            pltpu.VMEM((64, KC, 16, 128), BF),
            pltpu.VMEM((NB, 256, 128), BF),
            pltpu.VMEM((NB, T_LOCAL, HD), BF),
            pltpu.VMEM((NB, T_LOCAL, HD), BF),
            pltpu.VMEM((2, 256, T_LOCAL), F32),
            pltpu.VMEM((KC, 8, 128), F32),
            pltpu.SemaphoreType.DMA,
            pltpu.SemaphoreType.DMA((NB,)),
            pltpu.SemaphoreType.DMA((NB,)),
        ],
        compiler_params=pltpu.CompilerParams(vmem_limit_bytes=60 * 2**20),
        cost_estimate=pl.CostEstimate(flops=4 * 10**9, bytes_accessed=9 * 2**20, transcendentals=2**22),
        name=f"prefix{chunk}",
    )(order, q, swap, tail, keys, values)


def project_kernel(chunk, col_ref, r_ref, pm_ref, u_ref, *refs):
    last = chunk == CHUNKS - 1
    w_hbm, refs = refs[:8], refs[8:]
    if chunk:
        prev_ref, refs = refs[0], refs[1:]
    out_ref, wv, sem = refs[0], refs[-2], refs[-1]
    loads = [pltpu.make_async_copy(w_hbm[n].at[chunk], wv.at[n], sem.at[n]) for n in range(8)]
    for load in loads:
        load.start()
    f = lambda x: x.astype(F32)
    lp = f(r_ref[:, 136]) + f(r_ref[:, 137]) + f(r_ref[:, 138])
    lp = jnp.transpose(jnp.concatenate([lp, jnp.zeros((112, 128), F32)], 0))
    lane = iota((128, 128), 1)
    row = iota((128, 128), 0)
    cont = f(r_ref[:, 128:136]).reshape(128, 128)
    cols = jnp.zeros((128, 128), F32)
    for n in range(3):
        piece = jnp.broadcast_to(f(r_ref[:, 139 + n])[:, None, :], (16, 8, 128)).reshape(128, 128)
        piece = jnp.where(lane == row % 8, piece, 0.0).sum(1, keepdims=True)
        cols = cols + jnp.where(lane == n, jnp.broadcast_to(piece, (128, 128)), 0.0)
    moved = dot(pm_ref[...], jnp.concatenate([cont, cols], 1).astype(BF))
    lc = moved[:, 128:129] + moved[:, 129:130] + moved[:, 130:131]
    top = jnp.maximum(jnp.where(lane < 16, lp, -jnp.inf).max(1, keepdims=True), lc)
    wc = jnp.exp2(lc - top)
    wp = jnp.where(lane < 16, jnp.exp2(jnp.where(lane < 16, lp, top) - top), 0.0)
    den = wp.sum(1, keepdims=True) + wc
    num = wc * moved[:, :128]
    for src in range(16):
        num = num + wp[:, src : src + 1] * f(r_ref[src, :128])
    mixed = (num / den).astype(BF).reshape(4, 2, 16, 128)
    mixed = jnp.concatenate([mixed[:, 0].reshape(64, 128), mixed[:, 1].reshape(64, 128)], 1)
    mixed = dot(u_ref[...], mixed).astype(BF)
    y_ref = refs[1] if last else out_ref
    for n in range(8):
        at = pl.ds(pl.multiple_of(col_ref[n] * 512, 512), 512)
        loads[n].wait()
        y = dot(mixed, wv[n])
        if chunk:
            y = y + prev_ref[:, at]
        y_ref[:, at] = y
    if last:
        zf = refs[2]
        for quarter in range(4):
            block = y_ref[:, 1024 * quarter : 1024 * quarter + 1024]
            for dest in range(16):
                zf[dest, 4 * quarter : 4 * quarter + 4, :] = block[4 * dest : 4 * dest + 4]
        out_ref[...] = zf[...].astype(BF)


def project_call(chunk, columns, received, pm, unsort, weights, prev):
    args = (columns, received, pm, unsort, *weights) + ((prev,) if chunk else ())
    last = chunk == CHUNKS - 1
    scratch = [pltpu.VMEM((8, 2 * HD, 512), BF), pltpu.SemaphoreType.DMA((8,))]
    if last:
        out_shape = jax.ShapeDtypeStruct((16, 16, 1024), BF)
        scratch = [pltpu.VMEM((64, D), F32), pltpu.VMEM((16, 16, 1024), F32)] + scratch
    else:
        out_shape = jax.ShapeDtypeStruct((64, D), F32)
    return pl.pallas_call(
        functools.partial(project_kernel, chunk),
        out_shape=out_shape,
        in_specs=[SMEM, VMEM, VMEM, VMEM] + [ANY] * 8 + [VMEM] * (chunk > 0),
        out_specs=VMEM,
        scratch_shapes=scratch,
        compiler_params=pltpu.CompilerParams(vmem_limit_bytes=60 * 2**20),
        cost_estimate=pl.CostEstimate(flops=3 * 10**8, bytes_accessed=4 * 2**20, transcendentals=2**15),
        name=f"project{chunk}",
    )(*args)


def sum_kernel(r_ref, o_ref):
    total = r_ref[0].astype(F32)
    for src in range(1, 16):
        total = total + r_ref[src].astype(F32)
    for quarter in range(4):
        o_ref[:, 1024 * quarter : 1024 * quarter + 1024] = total[4 * quarter : 4 * quarter + 4].astype(BF)


def sum_call(received):
    return pl.pallas_call(
        sum_kernel,
        out_shape=jax.ShapeDtypeStruct((4, D), BF),
        in_specs=[VMEM],
        out_specs=VMEM,
        name="sum",
    )(received)


def spread_weights(w_out, seq):
    own = [
        lax.dynamic_slice_in_dim(w_out, (HC * c + 2 * seq) * HD, 2 * HD, 0) for c in range(CHUNKS)
    ]
    own = lax.optimization_barrier(jnp.stack(own))
    member = lax.axis_index("group")
    z, core = member // 2, member % 2
    blocks, columns = [own], [member]
    for k in (1, 2, 3):
        hop = [(2 * a + c, 2 * ((a + k) % 4) + c) for a in range(4) for c in range(2)]
        blocks.append(lax.ppermute(own, "group", hop))
        columns.append(2 * ((z - k) % 4) + core)
    swap = [(j, j ^ 1) for j in range(8)]
    blocks += [lax.ppermute(b, "group", swap) for b in blocks]
    columns += [c + 1 - 2 * core for c in columns]
    return blocks, jnp.stack(columns).astype(jnp.int32)


def per_device(
    queries, prefix_keys, prefix_values, cont_keys, cont_values, cont_len, prompt_of, w_out
):
    seq = lax.axis_index("seq")
    q = queries[0].reshape(4, HEADS, HD)
    q_rows = q.reshape(4 * HEADS, HD)
    copies = jnp.broadcast_to(q_rows[None], (16, 4 * HEADS, HD))
    copies, w_out = lax.optimization_barrier((copies, w_out))
    gathered = lax.all_to_all(copies, "seq", 0, 0).reshape(64, KVH, PER, HD)

    prompt = prompt_of[0]
    same = prompt[:, None] == prompt[None, :]
    earlier = jnp.arange(64)[None, :] < jnp.arange(64)[:, None]
    pos = prompt * SAMP + jnp.sum(same & earlier, axis=1, dtype=jnp.int32)
    unsort = pos[:, None] == jnp.arange(64)[None, :]
    order = jnp.sum(jnp.where(unsort, jnp.arange(64)[:, None], 0), axis=0, dtype=jnp.int32)
    r = jnp.arange(128)
    r_pos = (r // 32) * 16 + r % 16
    r_jj = (r // 16) % 2
    c_jj = (r // 4) % 2
    c_pos = jnp.repeat(pos.reshape(16, 1, 4), 2, axis=1).reshape(128)
    pm = ((r_pos[:, None] == c_pos[None, :]) & (r_jj[:, None] == c_jj[None, :])).astype(BF)
    unsort = unsort.astype(BF)
    swap = jnp.asarray(SWAP, BF)

    weights, columns = spread_weights(w_out, seq)
    tail = cont_call(cont_len[0], q, cont_keys[0], cont_values[0])
    received = []
    for c in range(CHUNKS):
        part = prefix_call(c, order, gathered, swap, tail, prefix_keys[0], prefix_values[0])
        received.append(lax.all_to_all(part, "seq", 0, 0))
    y = None
    for c in range(CHUNKS):
        y = project_call(c, columns, received[c], pm, unsort, weights, y)
    z = lax.all_to_all(y, "seq", 0, 0)
    return sum_call(z)[None]


def solution(mesh):
    return jax.shard_map(
        per_device,
        mesh=mesh,
        in_specs=(
            P("group", "seq", None),
            P("group", None, None, "seq", None),
            P("group", None, None, "seq", None),
            P("group", "seq", None, None, None),
            P("group", "seq", None, None, None),
            P("group", "seq"),
            P("group", None),
            P(None, "group"),
        ),
        out_specs=P("group", "seq", None),
        check_vma=False,
    )
```

```python
import jax
import jax.numpy as jnp
import numpy as np
from jax import lax
from jax.experimental import pallas as pl
from jax.experimental.pallas import tpu as pltpu
from jax.sharding import PartitionSpec as P

HEADS = 64
KVH = 4
HD = 128
PROMPTS = 4
SAMP = 16
DEST = 16
T_LOCAL = 2048
CONT = 512
D = 4096
ROWS = 288
TAIL_PITCH = 1024
LOG2E = float(np.log2(np.e))
SCALE2 = float(np.log2(np.e) / np.sqrt(HD))
BF = jnp.bfloat16
F32 = jnp.float32
VMEM = pl.BlockSpec(memory_space=pltpu.VMEM)
SMEM = pl.BlockSpec(memory_space=pltpu.SMEM)
ANY = pl.BlockSpec(memory_space=pl.ANY)
PARAMS = pltpu.CompilerParams(vmem_limit_bytes=60 * 2**20)


def dot(a, b):
    return jnp.dot(a, b, preferred_element_type=F32)


def dot_t(a, b):
    return lax.dot_general(a, b, (((1,), (1,)), ((), ())), preferred_element_type=F32)


def split3(x):
    hi = x.astype(BF).astype(F32)
    mid = (x - hi).astype(BF).astype(F32)
    return hi, mid, x - hi - mid


def iota(shape, dim):
    return lax.broadcasted_iota(jnp.int32, shape, dim)


def one_hot(mask):
    return jnp.where(mask, 1.0, 0.0).astype(BF)


def cont_kernel(
    len_ref, prompt_ref, q_ref, k_hbm, v_hbm, tail_hbm, pm_ref, un_ref, kb, vb, sb, wb, ob, tail_ref, sem, tsem
):
    loads = [pltpu.make_async_copy(k_hbm.at[s], kb.at[s], sem.at[s]) for s in range(4)]
    loads += [pltpu.make_async_copy(v_hbm.at[s], vb.at[s], sem.at[4 + s]) for s in range(4)]
    for load in loads:
        load.start()

    row, col = iota((64, 64), 0), iota((64, 64), 1)
    prompt = jnp.broadcast_to(prompt_ref[...].astype(F32), (64, 64))
    prompt_col = jnp.where(row == col, prompt, 0.0).sum(1, keepdims=True)
    before = jnp.where((prompt == prompt_col) & (col < row), 1.0, 0.0).sum(1, keepdims=True)
    place = prompt_col * SAMP + before
    here = jnp.broadcast_to(place, (64, 64)) == col.astype(F32)
    un_ref[...] = one_hot(here)
    place_row = jnp.where(row == col, jnp.broadcast_to(place, (64, 64)), 0.0).sum(0, keepdims=True)
    c64, r64 = iota((64, 256), 1), iota((64, 256), 0)
    pick = one_hot(r64 == 4 * (c64 >> 4) + (c64 & 3))
    place_c = dot(jnp.broadcast_to(place_row, (8, 64)).astype(BF), pick)[:1]
    r, c = iota((256, 256), 0), iota((256, 256), 1)
    wanted = ((r >> 6) * SAMP + (r & 15)).astype(F32)
    pm_ref[...] = one_hot(
        (jnp.broadcast_to(place_c, (256, 256)) == wanted) & (((r >> 4) & 3) == ((c >> 2) & 3))
    )

    for s in range(4):
        loads[s].wait()
        live = iota((64, CONT), 1) < len_ref[s]
        for k in range(KVH):
            at = 64 * s + 16 * k
            sb[at : at + 16] = dot_t(q_ref[at : at + 16], kb[s, k])
        sb[64 * s : 64 * s + 64] = jnp.where(live, sb[64 * s : 64 * s + 64], -jnp.inf)
    logit = sb[...]
    top = logit.max(1, keepdims=True)
    w = jnp.exp2((logit - top) * SCALE2)
    total = w.sum(1, keepdims=True)
    wb[...] = w.astype(BF)
    for s in range(4):
        loads[4 + s].wait()
        for k in range(KVH):
            at = 64 * s + 16 * k
            ob[at : at + 16] = dot(wb[at : at + 16], vb[s, k])
    o = ob[...] * (1.0 / total)
    lane = iota((256, 128), 1)
    terms = jnp.zeros((256, 128), F32)
    for n, part in enumerate(split3(top * SCALE2 + jnp.log(total) * LOG2E)):
        terms = terms + jnp.where(lane == n, jnp.broadcast_to(part, (256, 128)), 0.0)
    turn = one_hot(c == (r & 3) * 64 + (r >> 2))
    moved = dot(turn, jnp.concatenate([o, terms], 1).astype(BF))
    tail_ref[:, 16:32, :] = jnp.zeros((DEST, 16, 128), F32)
    tail_ref[:, :16, :] = moved[:, :128].reshape(DEST, 16, 128)
    r16 = iota((256, 128), 0) & 15
    for n in range(3):
        term = jnp.broadcast_to(moved[:, 128 + n : 129 + n], (256, 128))
        tail_ref[:, 22 + n, :] = jnp.where(lane == r16, term, 0.0).reshape(DEST, 16, 128).sum(1)
    send = pltpu.make_async_copy(tail_ref, tail_hbm.at[:, 0:32], tsem)
    send.start()
    send.wait()


def cont_call(lengths, prompt, q_rows, keys, values):
    return pl.pallas_call(
        cont_kernel,
        out_shape=(
            jax.ShapeDtypeStruct((DEST, TAIL_PITCH, 128), F32),
            jax.ShapeDtypeStruct((256, 256), BF),
            jax.ShapeDtypeStruct((64, 64), BF),
        ),
        in_specs=[SMEM, VMEM, VMEM, ANY, ANY],
        out_specs=(ANY, VMEM, VMEM),
        scratch_shapes=[
            pltpu.VMEM((4, KVH, CONT, HD), BF),
            pltpu.VMEM((4, KVH, CONT, HD), BF),
            pltpu.VMEM((256, CONT), F32),
            pltpu.VMEM((256, CONT), BF),
            pltpu.VMEM((256, HD), F32),
            pltpu.VMEM((DEST, 32, 128), F32),
            pltpu.SemaphoreType.DMA((8,)),
            pltpu.SemaphoreType.DMA,
        ],
        compiler_params=PARAMS,
        cost_estimate=pl.CostEstimate(flops=2 * 10**9, bytes_accessed=2**22, transcendentals=131072),
        name="cont",
    )(lengths, prompt, q_rows, keys, values)


NB = KVH * PROMPTS
TC = 512


GROUPS = ((0, 1), (1, 3), (3, 6), (6, 10), (10, 16))
AHEAD = 2


def prefix_kernel(
    prompt, qv, tail_hbm, k_hbm, v_hbm, o_hbm, qs, kb, vb, sbuf, st, tv, ov, order, seen, tsem, ks, vs, osem
):
    loads = []
    for b in range(NB):
        k, p = b // PROMPTS, b % PROMPTS
        loads.append(
            (
                pltpu.make_async_copy(k_hbm.at[p, k], kb.at[b], ks.at[b]),
                pltpu.make_async_copy(v_hbm.at[p, k], vb.at[b], vs.at[b]),
            )
        )
    load_tail = pltpu.make_async_copy(tail_hbm.at[:, 0:32], tv, tsem)

    def start(group):
        for b in range(*GROUPS[group]):
            for load in loads[b]:
                load.start()
        if group == 1:
            load_tail.start()

    for group in range(AHEAD):
        start(group)
    r, c = iota((256, 256), 0), iota((256, 256), 1)
    turn = one_hot(c == (r & 15) * 16 + (r >> 4))

    def gather(k):
        for p in range(PROMPTS):
            b = k * PROMPTS + p
            for i in range(SAMP):
                qs[b, 16 * i : 16 * i + 16] = qv[order[16 * p + i], k]
            qs[b] = dot(turn, qs[b]).astype(BF)

    row = iota((256, 128), 0) & 63
    lane = iota((256, 128), 1)
    spot = iota((4, 16, 128), 1)
    sends = []

    def finish(b, o, top, total):
        k, p = b // PROMPTS, b % PROMPTS
        at = slice(4 * k, 4 * k + 4)
        o = (o * (1.0 / total)).astype(BF)
        ov[at, 64 * p : 64 * p + 64, :] = o.reshape(4, 64, 128)
        lse = top * SCALE2 + jnp.log(total) * LOG2E
        part = jnp.where(lane == (p % 2) * 64 + row, jnp.broadcast_to(lse, (256, 128)), 0.0)
        part = part.reshape(4, 64, 128).sum(1)
        st[p // 2, k] = part if p % 2 == 0 else st[p // 2, k] + part
        if p == PROMPTS - 1:
            ov[at, 256:272, :] = tv[at, :16].astype(BF)
            tail = tv[at, 16:32]
            for half in range(2):
                for n, part in enumerate(split3(st[half, k])):
                    tail = jnp.where(spot == 2 * n + half, part[:, None, :], tail)
            ov[at, 272:288, :] = tail.astype(BF)
            send = pltpu.make_async_copy(ov.at[at], o_hbm.at[at], osem.at[k])
            send.start()
            sends.append(send)

    for p in range(PROMPTS):
        seen[p] = 0

    def place(n, carry):
        p = prompt[0, n]
        rank = seen[p]
        order[p * SAMP + rank] = n
        seen[p] = rank + 1
        return carry

    lax.fori_loop(0, 64, place, 0, unroll=8)
    gather(0)
    prev_top = None
    for b in range(NB + 1):
        peak = None
        if b < NB:
            if b == 3:
                load_tail.wait()
            for group, (first, last) in enumerate(GROUPS):
                if b == first:
                    for member in range(first, last):
                        for load in loads[member]:
                            load.wait()
                    if group + AHEAD < len(GROUPS):
                        start(group + AHEAD)
            if b in (3, 6, 10):
                gather({3: 1, 6: 2, 10: 3}[b])
            q = qs[b]
        if b > 0:
            acc = total = None
        for t in range(T_LOCAL // TC):
            cols = slice(t * TC, (t + 1) * TC)
            if b < NB:
                s = dot_t(q, kb[b, cols])
                sbuf[b % 2, :, cols] = s
                for z in range(TC // 128):
                    piece = s[:, 128 * z : 128 * z + 128]
                    peak = piece if peak is None else jnp.maximum(peak, piece)
            if b > 0:
                w = jnp.exp2((sbuf[(b - 1) % 2, :, cols] - prev_top) * SCALE2)
                for z in range(TC // 128):
                    piece = w[:, 128 * z : 128 * z + 128]
                    total = piece if total is None else total + piece
                o = dot(w.astype(BF), vb[b - 1, cols])
                acc = o if acc is None else acc + o
        if b > 0:
            finish(b - 1, acc, prev_top, total.sum(1, keepdims=True))
        if b < NB:
            prev_top = peak.max(1, keepdims=True)
    for send in sends:
        send.wait()


def prefix_call(prompt, q, tail, keys, values):
    return pl.pallas_call(
        prefix_kernel,
        out_shape=jax.ShapeDtypeStruct((DEST, ROWS, 128), BF),
        in_specs=[SMEM, VMEM, ANY, ANY, ANY],
        out_specs=ANY,
        scratch_shapes=[
            pltpu.VMEM((NB, 256, 128), BF),
            pltpu.VMEM((NB, T_LOCAL, HD), BF),
            pltpu.VMEM((NB, T_LOCAL, HD), BF),
            pltpu.VMEM((2, 256, T_LOCAL), F32),
            pltpu.VMEM((2, KVH, 4, 128), F32),
            pltpu.VMEM((DEST, 32, 128), F32),
            pltpu.VMEM((DEST, ROWS, 128), BF),
            pltpu.SMEM((64,), jnp.int32),
            pltpu.SMEM((PROMPTS,), jnp.int32),
            pltpu.SemaphoreType.DMA,
            pltpu.SemaphoreType.DMA((NB,)),
            pltpu.SemaphoreType.DMA((NB,)),
            pltpu.SemaphoreType.DMA((KVH,)),
        ],
        compiler_params=pltpu.CompilerParams(vmem_limit_bytes=50 * 2**20),
        cost_estimate=pl.CostEstimate(flops=9 * 10**9, bytes_accessed=18 * 2**20, transcendentals=2**23),
        name="prefix",
    )(prompt, q, tail, keys, values)


def pack_kernel(*refs):
    w_hbm, out_ref, sem = refs[:8], refs[8], refs[9]
    loads = [pltpu.make_async_copy(w_hbm[n], out_ref.at[n], sem.at[n]) for n in range(8)]
    for load in loads:
        load.start()
    for load in loads:
        load.wait()


def pack_call(weights):
    return pl.pallas_call(
        pack_kernel,
        out_shape=jax.ShapeDtypeStruct((8, 512, 512), BF),
        in_specs=[ANY] * 8,
        out_specs=ANY,
        scratch_shapes=[pltpu.SemaphoreType.DMA((8,))],
        compiler_params=pltpu.CompilerParams(vmem_limit_bytes=16 * 2**20),
        cost_estimate=pl.CostEstimate(flops=0, bytes_accessed=8 * 2**20, transcendentals=0),
        name="pack",
    )(*weights)


def project_kernel(r_ref, pm_ref, un_ref, w_hbm, z_ref, wv, yv, zf, wsem):
    loads = [pltpu.make_async_copy(w_hbm.at[n], wv.at[n], wsem.at[n]) for n in range(8)]
    for load in loads:
        load.start()
    f = lambda x: x.astype(F32)
    lane = iota((256, 128), 1)
    row = iota((256, 128), 0)
    pad = jnp.zeros((112, 128), F32)
    logs = []
    for half in range(2):
        part = f(r_ref[:, 272 + half]) + f(r_ref[:, 274 + half]) + f(r_ref[:, 276 + half])
        logs.append(jnp.transpose(jnp.concatenate([part, pad], 0)))
    logs = jnp.concatenate(logs, 0)
    cont = r_ref[:, 256:272].reshape(256, 128)
    terms = jnp.zeros((256, 128), F32)
    for n in range(3):
        term = jnp.broadcast_to(f(r_ref[:, 278 + n])[:, None, :], (16, 16, 128)).reshape(256, 128)
        term = jnp.where(lane == (row & 15), term, 0.0).sum(1, keepdims=True)
        terms = terms + jnp.where(lane == n, jnp.broadcast_to(term, (256, 128)), 0.0)
    moved = dot(pm_ref[...], jnp.concatenate([cont, terms.astype(BF)], 1))
    log_c = moved[:, 128:129] + moved[:, 129:130] + moved[:, 130:131]
    top = jnp.maximum(jnp.where(lane < 16, logs, -jnp.inf).max(1, keepdims=True), log_c)
    w_c = jnp.exp2(log_c - top)
    w_p = jnp.exp2(jnp.where(lane < 16, logs - top, -jnp.inf))
    den = w_p.sum(1, keepdims=True) + w_c
    num = w_c * moved[:, :128]
    for src in range(16):
        num = num + w_p[:, src : src + 1] * f(r_ref[src, :256])
    mixed = (num / den).astype(BF).reshape(4, 4, 16, 128)
    mixed = jnp.concatenate([mixed[:, jj].reshape(64, 128) for jj in range(4)], 1)
    mixed = dot(un_ref[...], mixed).astype(BF)
    member = lax.axis_index("group")
    z, core = member >> 1, member & 1
    for load in loads:
        load.wait()
    for n in range(8):
        g = 2 * ((z - n % 4) & 3) + (core if n < 4 else 1 - core)
        yv[g] = dot(mixed, wv[n])
    for g in range(8):
        cols = slice(512 * (g % 2), 512 * (g % 2) + 512)
        zf[:, 4 * (g // 2) : 4 * (g // 2) + 4, cols] = yv[g].reshape(DEST, 4, 512)
    z_ref[...] = zf[...].astype(BF)


def project_call(received, pm, unsort, weights):
    return pl.pallas_call(
        project_kernel,
        out_shape=jax.ShapeDtypeStruct((DEST, 16, 1024), BF),
        in_specs=[VMEM] * 3 + [ANY],
        out_specs=VMEM,
        scratch_shapes=[
            pltpu.VMEM((8, 512, 512), BF),
            pltpu.VMEM((8, 64, 512), F32),
            pltpu.VMEM((DEST, 16, 1024), F32),
            pltpu.SemaphoreType.DMA((8,)),
        ],
        compiler_params=pltpu.CompilerParams(vmem_limit_bytes=52 * 2**20),
        cost_estimate=pl.CostEstimate(flops=3 * 10**8, bytes_accessed=4 * 2**20, transcendentals=2**15),
        name="project",
    )(received, pm, unsort, weights)


def sum_kernel(r_ref, o_ref):
    total = r_ref[0].astype(F32)
    for src in range(1, DEST):
        total = total + r_ref[src].astype(F32)
    for quarter in range(4):
        o_ref[0, :, 1024 * quarter : 1024 * quarter + 1024] = total[
            4 * quarter : 4 * quarter + 4
        ].astype(BF)


def sum_call(received):
    return pl.pallas_call(
        sum_kernel,
        out_shape=jax.ShapeDtypeStruct((1, 4, D), BF),
        in_specs=[VMEM],
        out_specs=VMEM,
        compiler_params=pltpu.CompilerParams(vmem_limit_bytes=16 * 2**20),
        name="sum",
    )(received)


def gather_weights(w_out, seq):
    own = lax.optimization_barrier(lax.dynamic_slice_in_dim(w_out, 4 * seq * HD, 4 * HD, 0))
    blocks = [own]
    for k in (1, 2, 3):
        hop = [(2 * a + c, 2 * ((a + k) % 4) + c) for a in range(4) for c in range(2)]
        blocks.append(lax.ppermute(own, "group", hop))
    return blocks


def per_device(
    queries, prefix_keys, prefix_values, cont_keys, cont_values, cont_len, prompt_of, w_out
):
    q_rows = queries.reshape(4 * HEADS, HD)
    copies = jnp.broadcast_to(q_rows[None], (DEST, 4 * HEADS, HD))
    copies, w_out = lax.optimization_barrier((copies, w_out))
    gathered = lax.all_to_all(copies, "seq", 0, 0).reshape(64, KVH, 16, HD)
    weights = gather_weights(w_out, lax.axis_index("seq"))
    tail, pm, unsort = cont_call(cont_len[0], prompt_of, q_rows, cont_keys[0], cont_values[0])
    part = prefix_call(prompt_of, gathered, tail, prefix_keys[0], prefix_values[0])
    part, weights = lax.optimization_barrier((part, weights))
    swap = [(j, j ^ 1) for j in range(8)]
    weights = weights + [lax.ppermute(b, "group", swap) for b in weights]
    received = lax.all_to_all(part, "seq", 0, 0)
    y = project_call(received, pm, unsort, pack_call(weights))
    return sum_call(lax.all_to_all(y, "seq", 0, 0))


def solution(mesh):
    return jax.shard_map(
        per_device,
        mesh=mesh,
        in_specs=(
            P("group", "seq", None),
            P("group", None, None, "seq", None),
            P("group", None, None, "seq", None),
            P("group", "seq", None, None, None),
            P("group", "seq", None, None, None),
            P("group", "seq"),
            P("group", None),
            P(None, "group"),
        ),
        out_specs=P("group", "seq", None),
        check_vma=False,
    )
```

```python
import jax
import jax.numpy as jnp
import numpy as np
from jax import lax
from jax.experimental import pallas as pl
from jax.experimental.pallas import tpu as pltpu
from jax.sharding import PartitionSpec as P

HEADS = 64
KVH = 4
HD = 128
PROMPTS = 4
SAMP = 16
DEST = 16
T_LOCAL = 2048
CONT = 512
D = 4096
ROWS = 288
TAIL_PITCH = 1024
LOG2E = float(np.log2(np.e))
SCALE2 = float(np.log2(np.e) / np.sqrt(HD))
BF = jnp.bfloat16
F32 = jnp.float32
VMEM = pl.BlockSpec(memory_space=pltpu.VMEM)
SMEM = pl.BlockSpec(memory_space=pltpu.SMEM)
ANY = pl.BlockSpec(memory_space=pl.ANY)
PARAMS = pltpu.CompilerParams(vmem_limit_bytes=60 * 2**20)


def dot(a, b):
    return jnp.dot(a, b, preferred_element_type=F32)


def dot_t(a, b):
    return lax.dot_general(a, b, (((1,), (1,)), ((), ())), preferred_element_type=F32)


def split3(x):
    hi = x.astype(BF).astype(F32)
    mid = (x - hi).astype(BF).astype(F32)
    return hi, mid, x - hi - mid


def iota(shape, dim):
    return lax.broadcasted_iota(jnp.int32, shape, dim)


def one_hot(mask):
    return jnp.where(mask, 1.0, 0.0).astype(BF)


def copies_kernel(q_ref, out_hbm, sem):
    sends = [pltpu.make_async_copy(q_ref.at[0], out_hbm.at[d], sem.at[d]) for d in range(DEST)]
    for send in sends:
        send.start()
    for send in sends:
        send.wait()


def copies_call(queries):
    return pl.pallas_call(
        copies_kernel,
        out_shape=jax.ShapeDtypeStruct((DEST, 4, HEADS * HD), BF),
        in_specs=[VMEM],
        out_specs=ANY,
        scratch_shapes=[pltpu.SemaphoreType.DMA((DEST,))],
        compiler_params=PARAMS,
        name="copies",
    )(queries)


def place_of(prompt):
    row, col = iota((64, 64), 0), iota((64, 64), 1)
    prompt = jnp.broadcast_to(prompt.astype(F32), (64, 64))
    prompt_col = jnp.where(row == col, prompt, 0.0).sum(1, keepdims=True)
    before = jnp.where((prompt == prompt_col) & (col < row), 1.0, 0.0).sum(1, keepdims=True)
    return jnp.broadcast_to(prompt_col * SAMP + before, (64, 64))


def as_row(column):
    row, col = iota((64, 64), 0), iota((64, 64), 1)
    return jnp.where(row == col, column, 0.0).sum(0, keepdims=True)


def cont_kernel(
    len_ref, prompt_ref, q_in, k_hbm, v_hbm, tail_hbm, pm_ref, un_ref, kb, vb, sb, wb, ob, tail_ref, qf, q_ref, sem, tsem
):
    loads = [pltpu.make_async_copy(k_hbm.at[s], kb.at[s], sem.at[s]) for s in range(4)]
    loads += [pltpu.make_async_copy(v_hbm.at[s], vb.at[s], sem.at[4 + s]) for s in range(4)]
    for load in loads:
        load.start()

    for h in range(HEADS):
        qf[pl.ds(h, 4, stride=HEADS), :] = q_in[0, :, HD * h : HD * h + HD].astype(F32)
    q_ref[...] = qf[...].astype(BF)

    place = place_of(prompt_ref[...])
    un_ref[...] = one_hot(place == iota((64, 64), 1).astype(F32))
    place_row = as_row(place)
    c64, r64 = iota((64, 256), 1), iota((64, 256), 0)
    pick = one_hot(r64 == 4 * (c64 >> 4) + (c64 & 3))
    place_c = dot(jnp.broadcast_to(place_row, (8, 64)).astype(BF), pick)[:1]
    r, c = iota((256, 256), 0), iota((256, 256), 1)
    wanted = ((r >> 6) * SAMP + (r & 15)).astype(F32)
    pm_ref[...] = one_hot(
        (jnp.broadcast_to(place_c, (256, 256)) == wanted) & (((r >> 4) & 3) == ((c >> 2) & 3))
    )

    for s in range(4):
        loads[s].wait()
        live = iota((64, CONT), 1) < len_ref[s]
        for k in range(KVH):
            at = 64 * s + 16 * k
            sb[at : at + 16] = dot_t(q_ref[at : at + 16], kb[s, k])
        sb[64 * s : 64 * s + 64] = jnp.where(live, sb[64 * s : 64 * s + 64], -jnp.inf)
    logit = sb[...]
    top = logit.max(1, keepdims=True)
    w = jnp.exp2((logit - top) * SCALE2)
    total = w.sum(1, keepdims=True)
    wb[...] = w.astype(BF)
    for s in range(4):
        loads[4 + s].wait()
        for k in range(KVH):
            at = 64 * s + 16 * k
            ob[at : at + 16] = dot(wb[at : at + 16], vb[s, k])
    o = ob[...] * (1.0 / total)
    lane = iota((256, 128), 1)
    terms = jnp.zeros((256, 128), F32)
    for n, part in enumerate(split3(top * SCALE2 + jnp.log(total) * LOG2E)):
        terms = terms + jnp.where(lane == n, jnp.broadcast_to(part, (256, 128)), 0.0)
    turn = one_hot(c == (r & 3) * 64 + (r >> 2))
    moved = dot(turn, jnp.concatenate([o, terms], 1).astype(BF))
    tail_ref[:, 16:32, :] = jnp.zeros((DEST, 16, 128), F32)
    tail_ref[:, :16, :] = moved[:, :128].reshape(DEST, 16, 128)
    r16 = iota((256, 128), 0) & 15
    for n in range(3):
        term = jnp.broadcast_to(moved[:, 128 + n : 129 + n], (256, 128))
        tail_ref[:, 22 + n, :] = jnp.where(lane == r16, term, 0.0).reshape(DEST, 16, 128).sum(1)
    send = pltpu.make_async_copy(tail_ref, tail_hbm.at[:, 0:32], tsem)
    send.start()
    send.wait()


def cont_call(lengths, prompt, queries, keys, values):
    return pl.pallas_call(
        cont_kernel,
        out_shape=(
            jax.ShapeDtypeStruct((DEST, TAIL_PITCH, 128), F32),
            jax.ShapeDtypeStruct((256, 256), BF),
            jax.ShapeDtypeStruct((64, 64), BF),
        ),
        in_specs=[SMEM, VMEM, VMEM, ANY, ANY],
        out_specs=(ANY, VMEM, VMEM),
        scratch_shapes=[
            pltpu.VMEM((4, KVH, CONT, HD), BF),
            pltpu.VMEM((4, KVH, CONT, HD), BF),
            pltpu.VMEM((256, CONT), F32),
            pltpu.VMEM((256, CONT), BF),
            pltpu.VMEM((256, HD), F32),
            pltpu.VMEM((DEST, 32, 128), F32),
            pltpu.VMEM((256, HD), F32),
            pltpu.VMEM((256, HD), BF),
            pltpu.SemaphoreType.DMA((8,)),
            pltpu.SemaphoreType.DMA,
        ],
        compiler_params=PARAMS,
        cost_estimate=pl.CostEstimate(flops=2 * 10**9, bytes_accessed=2**22, transcendentals=131072),
        name="cont",
    )(lengths, prompt, queries, keys, values)


NB = KVH * PROMPTS
TC = 512


GROUPS = ((0, 2), (2, 6), (6, 16))
AHEAD = 2


def prefix_kernel(
    prompt, q_ref, tail_hbm, k_hbm, v_hbm, o_hbm, qs, kb, vb, sbuf, st, tv, ov, qf, qb, tsem, ks, vs, osem
):
    loads = []
    for first, last in GROUPS:
        loads.append([])
        while first < last:
            k, p = first // PROMPTS, first % PROMPTS
            stop = min(last, (k + 1) * PROMPTS)
            for hbm, buf, sem in ((k_hbm, kb, ks), (v_hbm, vb, vs)):
                source = hbm.at[p : p + stop - first, k]
                loads[-1].append(pltpu.make_async_copy(source, buf.at[first:stop], sem.at[first]))
            first = stop
    load_tail = pltpu.make_async_copy(tail_hbm.at[:, 0:32], tv, tsem)

    def start(group):
        for load in loads[group]:
            load.start()
        if group == 1:
            load_tail.start()

    for group in range(AHEAD):
        start(group)
    sort = one_hot(as_row(place_of(prompt[...])) == iota((64, 64), 0).astype(F32))
    for d in range(DEST):
        qf[4 * d : 4 * d + 4, :] = q_ref[d].astype(F32)
    qb[...] = qf[...].astype(BF)

    def gather(k):
        ordered = dot(sort, qb[:, 2048 * k : 2048 * k + 2048]).astype(BF)
        for p in range(PROMPTS):
            for j in range(16):
                piece = ordered[16 * p : 16 * p + 16, 128 * j : 128 * j + 128]
                qs[k * PROMPTS + p, 16 * j : 16 * j + 16] = piece

    row = iota((256, 128), 0) & 63
    lane = iota((256, 128), 1)
    spot = iota((4, 16, 128), 1)
    sends = []

    def finish(b, o, top, total):
        k, p = b // PROMPTS, b % PROMPTS
        at = slice(4 * k, 4 * k + 4)
        o = (o * (1.0 / total)).astype(BF)
        ov[at, 64 * p : 64 * p + 64, :] = o.reshape(4, 64, 128)
        lse = top * SCALE2 + jnp.log(total) * LOG2E
        part = jnp.where(lane == (p % 2) * 64 + row, jnp.broadcast_to(lse, (256, 128)), 0.0)
        part = part.reshape(4, 64, 128).sum(1)
        st[p // 2, k] = part if p % 2 == 0 else st[p // 2, k] + part
        if p == PROMPTS - 1:
            ov[at, 256:272, :] = tv[at, :16].astype(BF)
            tail = tv[at, 16:32]
            for half in range(2):
                for n, part in enumerate(split3(st[half, k])):
                    tail = jnp.where(spot == 2 * n + half, part[:, None, :], tail)
            ov[at, 272:288, :] = tail.astype(BF)
            send = pltpu.make_async_copy(ov.at[at], o_hbm.at[at], osem.at[k])
            send.start()
            sends.append(send)

    gather(0)
    prev_top = None
    for b in range(NB + 1):
        peak = None
        if b < NB:
            if b == 2:
                load_tail.wait()
            for group, (first, last) in enumerate(GROUPS):
                if b == first:
                    for load in loads[group]:
                        load.wait()
                    if group + AHEAD < len(GROUPS):
                        start(group + AHEAD)
            if b in (2, 6, 8):
                gather({2: 1, 6: 2, 8: 3}[b])
            q = qs[b]
        if b > 0:
            acc = total = None
        for t in range(T_LOCAL // TC):
            cols = slice(t * TC, (t + 1) * TC)
            if b < NB:
                s = dot_t(q, kb[b, cols])
                sbuf[b % 2, :, cols] = s
                for z in range(TC // 128):
                    piece = s[:, 128 * z : 128 * z + 128]
                    peak = piece if peak is None else jnp.maximum(peak, piece)
            if b > 0:
                w = jnp.exp2((sbuf[(b - 1) % 2, :, cols] - prev_top) * SCALE2)
                for z in range(TC // 128):
                    piece = w[:, 128 * z : 128 * z + 128]
                    total = piece if total is None else total + piece
                o = dot(w.astype(BF), vb[b - 1, cols])
                acc = o if acc is None else acc + o
        if b > 0:
            finish(b - 1, acc, prev_top, total.sum(1, keepdims=True))
        if b < NB:
            prev_top = peak.max(1, keepdims=True)
    for send in sends:
        send.wait()


def prefix_call(prompt, q, tail, keys, values):
    return pl.pallas_call(
        prefix_kernel,
        out_shape=jax.ShapeDtypeStruct((DEST, ROWS, 128), BF),
        in_specs=[VMEM, VMEM, ANY, ANY, ANY],
        out_specs=ANY,
        scratch_shapes=[
            pltpu.VMEM((NB, 256, 128), BF),
            pltpu.VMEM((NB, T_LOCAL, HD), BF),
            pltpu.VMEM((NB, T_LOCAL, HD), BF),
            pltpu.VMEM((2, 256, T_LOCAL), F32),
            pltpu.VMEM((2, KVH, 4, 128), F32),
            pltpu.VMEM((DEST, 32, 128), F32),
            pltpu.VMEM((DEST, ROWS, 128), BF),
            pltpu.VMEM((64, HEADS * HD), F32),
            pltpu.VMEM((64, HEADS * HD), BF),
            pltpu.SemaphoreType.DMA,
            pltpu.SemaphoreType.DMA((NB,)),
            pltpu.SemaphoreType.DMA((NB,)),
            pltpu.SemaphoreType.DMA((KVH,)),
        ],
        compiler_params=pltpu.CompilerParams(vmem_limit_bytes=50 * 2**20),
        cost_estimate=pl.CostEstimate(flops=9 * 10**9, bytes_accessed=18 * 2**20, transcendentals=2**23),
        name="prefix",
    )(prompt, q, tail, keys, values)


def pack_kernel(*refs):
    w_hbm, out_ref, sem = refs[:8], refs[8], refs[9]
    loads = [pltpu.make_async_copy(w_hbm[n], out_ref.at[n], sem.at[n]) for n in range(8)]
    for load in loads:
        load.start()
    for load in loads:
        load.wait()


def pack_call(weights):
    return pl.pallas_call(
        pack_kernel,
        out_shape=jax.ShapeDtypeStruct((8, 512, 512), BF),
        in_specs=[ANY] * 8,
        out_specs=ANY,
        scratch_shapes=[pltpu.SemaphoreType.DMA((8,))],
        compiler_params=pltpu.CompilerParams(vmem_limit_bytes=16 * 2**20),
        cost_estimate=pl.CostEstimate(flops=0, bytes_accessed=8 * 2**20, transcendentals=0),
        name="pack",
    )(*weights)


def project_kernel(r_ref, pm_ref, un_ref, w_hbm, z_ref, wv, yv, zf, wsem):
    loads = [pltpu.make_async_copy(w_hbm.at[n], wv.at[n], wsem.at[n]) for n in range(8)]
    for load in loads[:4]:
        load.start()
    f = lambda x: x.astype(F32)
    lane = iota((256, 128), 1)
    row = iota((256, 128), 0)
    pad = jnp.zeros((112, 128), F32)
    logs = []
    for half in range(2):
        part = f(r_ref[:, 272 + half]) + f(r_ref[:, 274 + half]) + f(r_ref[:, 276 + half])
        logs.append(jnp.transpose(jnp.concatenate([part, pad], 0)))
    logs = jnp.concatenate(logs, 0)
    cont = r_ref[:, 256:272].reshape(256, 128)
    terms = jnp.zeros((256, 128), F32)
    for n in range(3):
        term = jnp.broadcast_to(f(r_ref[:, 278 + n])[:, None, :], (16, 16, 128)).reshape(256, 128)
        term = jnp.where(lane == (row & 15), term, 0.0).sum(1, keepdims=True)
        terms = terms + jnp.where(lane == n, jnp.broadcast_to(term, (256, 128)), 0.0)
    moved = dot(pm_ref[...], jnp.concatenate([cont, terms.astype(BF)], 1))
    for load in loads[:4]:
        load.wait()
    for load in loads[4:]:
        load.start()
    log_c = moved[:, 128:129] + moved[:, 129:130] + moved[:, 130:131]
    top = jnp.maximum(jnp.where(lane < 16, logs, -jnp.inf).max(1, keepdims=True), log_c)
    w_c = jnp.exp2(log_c - top)
    w_p = jnp.exp2(jnp.where(lane < 16, logs - top, -jnp.inf))
    den = w_p.sum(1, keepdims=True) + w_c
    num = w_c * moved[:, :128]
    for src in range(16):
        num = num + w_p[:, src : src + 1] * f(r_ref[src, :256])
    mixed = (num / den).astype(BF).reshape(4, 4, 16, 128)
    mixed = jnp.concatenate([mixed[:, jj].reshape(64, 128) for jj in range(4)], 1)
    mixed = dot(un_ref[...], mixed).astype(BF)
    member = lax.axis_index("group")
    z, core = member >> 1, member & 1
    for n in range(8):
        if n == 4:
            for load in loads[4:]:
                load.wait()
        g = 2 * ((z - n % 4) & 3) + (core if n < 4 else 1 - core)
        yv[g] = dot(mixed, wv[n])
    for g in range(8):
        cols = slice(512 * (g % 2), 512 * (g % 2) + 512)
        zf[:, 4 * (g // 2) : 4 * (g // 2) + 4, cols] = yv[g].reshape(DEST, 4, 512)
    z_ref[...] = zf[...].astype(BF)


def project_call(received, pm, unsort, weights):
    return pl.pallas_call(
        project_kernel,
        out_shape=jax.ShapeDtypeStruct((DEST, 16, 1024), BF),
        in_specs=[VMEM] * 3 + [ANY],
        out_specs=VMEM,
        scratch_shapes=[
            pltpu.VMEM((8, 512, 512), BF),
            pltpu.VMEM((8, 64, 512), F32),
            pltpu.VMEM((DEST, 16, 1024), F32),
            pltpu.SemaphoreType.DMA((8,)),
        ],
        compiler_params=pltpu.CompilerParams(vmem_limit_bytes=52 * 2**20),
        cost_estimate=pl.CostEstimate(flops=3 * 10**8, bytes_accessed=4 * 2**20, transcendentals=2**15),
        name="project",
    )(received, pm, unsort, weights)


def sum_kernel(r_ref, o_ref):
    total = r_ref[0].astype(F32)
    for src in range(1, DEST):
        total = total + r_ref[src].astype(F32)
    for quarter in range(4):
        o_ref[0, :, 1024 * quarter : 1024 * quarter + 1024] = total[
            4 * quarter : 4 * quarter + 4
        ].astype(BF)


def sum_call(received):
    return pl.pallas_call(
        sum_kernel,
        out_shape=jax.ShapeDtypeStruct((1, 4, D), BF),
        in_specs=[VMEM],
        out_specs=VMEM,
        compiler_params=pltpu.CompilerParams(vmem_limit_bytes=16 * 2**20),
        name="sum",
    )(received)


def gather_weights(w_out, seq):
    own = lax.optimization_barrier(lax.dynamic_slice_in_dim(w_out, 4 * seq * HD, 4 * HD, 0))
    blocks = [own]
    for k in (1, 2, 3):
        hop = [(2 * a + c, 2 * ((a + k) % 4) + c) for a in range(4) for c in range(2)]
        blocks.append(lax.ppermute(own, "group", hop))
    return blocks


def per_device(
    queries, prefix_keys, prefix_values, cont_keys, cont_values, cont_len, prompt_of, w_out
):
    copies = copies_call(queries)
    copies, w_out = lax.optimization_barrier((copies, w_out))
    gathered = lax.all_to_all(copies, "seq", 0, 0)
    weights = gather_weights(w_out, lax.axis_index("seq"))
    tail, pm, unsort = cont_call(cont_len[0], prompt_of, queries, cont_keys[0], cont_values[0])
    part = prefix_call(prompt_of, gathered, tail, prefix_keys[0], prefix_values[0])
    part, weights = lax.optimization_barrier((part, weights))
    swap = [(j, j ^ 1) for j in range(8)]
    weights = weights + [lax.ppermute(b, "group", swap) for b in weights]
    received = lax.all_to_all(part, "seq", 0, 0)
    y = project_call(received, pm, unsort, pack_call(weights))
    return sum_call(lax.all_to_all(y, "seq", 0, 0))


def solution(mesh):
    return jax.shard_map(
        per_device,
        mesh=mesh,
        in_specs=(
            P("group", "seq", None),
            P("group", None, None, "seq", None),
            P("group", None, None, "seq", None),
            P("group", "seq", None, None, None),
            P("group", "seq", None, None, None),
            P("group", "seq"),
            P("group", None),
            P(None, "group"),
        ),
        out_specs=P("group", "seq", None),
        check_vma=False,
    )
```

```python
import jax
import jax.numpy as jnp
import numpy as np
from jax import lax
from jax.experimental import pallas as pl
from jax.experimental.pallas import tpu as pltpu
from jax.sharding import PartitionSpec as P

HEADS = 64
KVH = 4
HD = 128
PROMPTS = 4
SAMP = 16
DEST = 16
T_LOCAL = 2048
CONT = 512
D = 4096
ROWS = 288
TAIL_PITCH = 1024
LOG2E = float(np.log2(np.e))
SCALE2 = float(np.log2(np.e) / np.sqrt(HD))
BF = jnp.bfloat16
F32 = jnp.float32
VMEM = pl.BlockSpec(memory_space=pltpu.VMEM)
SMEM = pl.BlockSpec(memory_space=pltpu.SMEM)
ANY = pl.BlockSpec(memory_space=pl.ANY)
PARAMS = pltpu.CompilerParams(vmem_limit_bytes=60 * 2**20)


def dot(a, b):
    return jnp.dot(a, b, preferred_element_type=F32)


def dot_t(a, b):
    return lax.dot_general(a, b, (((1,), (1,)), ((), ())), preferred_element_type=F32)


def split3(x):
    hi = x.astype(BF).astype(F32)
    mid = (x - hi).astype(BF).astype(F32)
    return hi, mid, x - hi - mid


def iota(shape, dim):
    return lax.broadcasted_iota(jnp.int32, shape, dim)


def one_hot(mask):
    return jnp.where(mask, 1.0, 0.0).astype(BF)


def copies_kernel(q_ref, out_hbm, sem):
    sends = [pltpu.make_async_copy(q_ref.at[0], out_hbm.at[d], sem.at[d]) for d in range(DEST)]
    for send in sends:
        send.start()
    for send in sends:
        send.wait()


def copies_call(queries):
    return pl.pallas_call(
        copies_kernel,
        out_shape=jax.ShapeDtypeStruct((DEST, 4, HEADS * HD), BF),
        in_specs=[VMEM],
        out_specs=ANY,
        scratch_shapes=[pltpu.SemaphoreType.DMA((DEST,))],
        compiler_params=PARAMS,
        name="copies",
    )(queries)


def place_of(prompt):
    row, col = iota((64, 64), 0), iota((64, 64), 1)
    prompt = jnp.broadcast_to(prompt.astype(F32), (64, 64))
    prompt_col = jnp.where(row == col, prompt, 0.0).sum(1, keepdims=True)
    before = jnp.where((prompt == prompt_col) & (col < row), 1.0, 0.0).sum(1, keepdims=True)
    return jnp.broadcast_to(prompt_col * SAMP + before, (64, 64))


def as_row(column):
    row, col = iota((64, 64), 0), iota((64, 64), 1)
    return jnp.where(row == col, column, 0.0).sum(0, keepdims=True)


def cont_kernel(
    len_ref, prompt_ref, q_in, k_hbm, v_hbm, tail_hbm, pm_ref, un_ref, kb, vb, sb, wb, ob, tail_ref, qf, q_ref, sem, tsem
):
    loads = [pltpu.make_async_copy(k_hbm.at[s], kb.at[s], sem.at[s]) for s in range(4)]
    loads += [pltpu.make_async_copy(v_hbm.at[s], vb.at[s], sem.at[4 + s]) for s in range(4)]
    for load in loads:
        load.start()

    for h in range(HEADS):
        qf[pl.ds(h, 4, stride=HEADS), :] = q_in[0, :, HD * h : HD * h + HD].astype(F32)
    q_ref[...] = qf[...].astype(BF)

    place = place_of(prompt_ref[...])
    un_ref[...] = one_hot(place == iota((64, 64), 1).astype(F32))
    place_row = as_row(place)
    c64, r64 = iota((64, 256), 1), iota((64, 256), 0)
    pick = one_hot(r64 == 4 * (c64 >> 4) + (c64 & 3))
    place_c = dot(jnp.broadcast_to(place_row, (8, 64)).astype(BF), pick)[:1]
    r, c = iota((256, 256), 0), iota((256, 256), 1)
    wanted = ((r >> 6) * SAMP + (r & 15)).astype(F32)
    pm_ref[...] = one_hot(
        (jnp.broadcast_to(place_c, (256, 256)) == wanted) & (((r >> 4) & 3) == ((c >> 2) & 3))
    )

    for s in range(4):
        loads[s].wait()
        live = iota((64, CONT), 1) < len_ref[s]
        for k in range(KVH):
            at = 64 * s + 16 * k
            sb[at : at + 16] = dot_t(q_ref[at : at + 16], kb[s, k])
        sb[64 * s : 64 * s + 64] = jnp.where(live, sb[64 * s : 64 * s + 64], -jnp.inf)
    logit = sb[...]
    top = logit.max(1, keepdims=True)
    w = jnp.exp2((logit - top) * SCALE2)
    total = w.sum(1, keepdims=True)
    wb[...] = w.astype(BF)
    for s in range(4):
        loads[4 + s].wait()
        for k in range(KVH):
            at = 64 * s + 16 * k
            ob[at : at + 16] = dot(wb[at : at + 16], vb[s, k])
    o = ob[...] * (1.0 / total)
    lane = iota((256, 128), 1)
    terms = jnp.zeros((256, 128), F32)
    for n, part in enumerate(split3(top * SCALE2 + jnp.log(total) * LOG2E)):
        terms = terms + jnp.where(lane == n, jnp.broadcast_to(part, (256, 128)), 0.0)
    turn = one_hot(c == (r & 3) * 64 + (r >> 2))
    moved = dot(turn, jnp.concatenate([o, terms], 1).astype(BF))
    tail_ref[:, 16:32, :] = jnp.zeros((DEST, 16, 128), F32)
    tail_ref[:, :16, :] = moved[:, :128].reshape(DEST, 16, 128)
    r16 = iota((256, 128), 0) & 15
    for n in range(3):
        term = jnp.broadcast_to(moved[:, 128 + n : 129 + n], (256, 128))
        tail_ref[:, 22 + n, :] = jnp.where(lane == r16, term, 0.0).reshape(DEST, 16, 128).sum(1)
    send = pltpu.make_async_copy(tail_ref, tail_hbm.at[:, 0:32], tsem)
    send.start()
    send.wait()


def cont_call(lengths, prompt, queries, keys, values):
    return pl.pallas_call(
        cont_kernel,
        out_shape=(
            jax.ShapeDtypeStruct((DEST, TAIL_PITCH, 128), F32),
            jax.ShapeDtypeStruct((256, 256), BF),
            jax.ShapeDtypeStruct((64, 64), BF),
        ),
        in_specs=[SMEM, VMEM, VMEM, ANY, ANY],
        out_specs=(ANY, VMEM, VMEM),
        scratch_shapes=[
            pltpu.VMEM((4, KVH, CONT, HD), BF),
            pltpu.VMEM((4, KVH, CONT, HD), BF),
            pltpu.VMEM((256, CONT), F32),
            pltpu.VMEM((256, CONT), BF),
            pltpu.VMEM((256, HD), F32),
            pltpu.VMEM((DEST, 32, 128), F32),
            pltpu.VMEM((256, HD), F32),
            pltpu.VMEM((256, HD), BF),
            pltpu.SemaphoreType.DMA((8,)),
            pltpu.SemaphoreType.DMA,
        ],
        compiler_params=PARAMS,
        cost_estimate=pl.CostEstimate(flops=2 * 10**9, bytes_accessed=2**22, transcendentals=131072),
        name="cont",
    )(lengths, prompt, queries, keys, values)


NB = KVH * PROMPTS
TC = 512


GROUPS = ((0, 2), (2, 6), (6, 16))
AHEAD = 2


def prefix_kernel(
    prompt, q_ref, tail_hbm, k_hbm, v_hbm, o_hbm, qs, kb, vb, sbuf, st, tv, ov, qf, qb, tsem, ks, vs, osem
):
    loads = []
    for first, last in GROUPS:
        loads.append([])
        while first < last:
            k, p = first // PROMPTS, first % PROMPTS
            stop = min(last, (k + 1) * PROMPTS)
            for hbm, buf, sem in ((k_hbm, kb, ks), (v_hbm, vb, vs)):
                source = hbm.at[p : p + stop - first, k]
                loads[-1].append(pltpu.make_async_copy(source, buf.at[first:stop], sem.at[first]))
            first = stop
    load_tail = pltpu.make_async_copy(tail_hbm.at[:, 0:32], tv, tsem)

    def start(group):
        for load in loads[group]:
            load.start()
        if group == 1:
            load_tail.start()

    for group in range(AHEAD):
        start(group)
    sort = one_hot(as_row(place_of(prompt[...])) == iota((64, 64), 0).astype(F32))
    for d in range(DEST):
        qf[4 * d : 4 * d + 4, :] = q_ref[d].astype(F32)
    qb[...] = qf[...].astype(BF)

    def gather(k):
        ordered = dot(sort, qb[:, 2048 * k : 2048 * k + 2048]).astype(BF)
        for p in range(PROMPTS):
            for j in range(16):
                piece = ordered[16 * p : 16 * p + 16, 128 * j : 128 * j + 128]
                qs[k * PROMPTS + p, 16 * j : 16 * j + 16] = piece

    row = iota((256, 128), 0) & 63
    lane = iota((256, 128), 1)
    spot = iota((4, 16, 128), 1)
    sends = []

    def finish(b, o, top, total):
        k, p = b // PROMPTS, b % PROMPTS
        at = slice(4 * k, 4 * k + 4)
        o = (o * (1.0 / total)).astype(BF)
        ov[at, 64 * p : 64 * p + 64, :] = o.reshape(4, 64, 128)
        lse = top * SCALE2 + jnp.log(total) * LOG2E
        part = jnp.where(lane == (p % 2) * 64 + row, jnp.broadcast_to(lse, (256, 128)), 0.0)
        part = part.reshape(4, 64, 128).sum(1)
        st[p // 2, k] = part if p % 2 == 0 else st[p // 2, k] + part
        if p == PROMPTS - 1:
            ov[at, 256:272, :] = tv[at, :16].astype(BF)
            tail = tv[at, 16:32]
            for half in range(2):
                for n, part in enumerate(split3(st[half, k])):
                    tail = jnp.where(spot == 2 * n + half, part[:, None, :], tail)
            ov[at, 272:288, :] = tail.astype(BF)
            send = pltpu.make_async_copy(ov.at[at], o_hbm.at[at], osem.at[k])
            send.start()
            sends.append(send)

    gather(0)
    prev_top = None
    for b in range(NB + 1):
        peak = None
        if b < NB:
            if b == 2:
                load_tail.wait()
            for group, (first, last) in enumerate(GROUPS):
                if b == first:
                    for load in loads[group]:
                        load.wait()
                    if group + AHEAD < len(GROUPS):
                        start(group + AHEAD)
            if b in (2, 6, 8):
                gather({2: 1, 6: 2, 8: 3}[b])
            q = qs[b]
        if b > 0:
            acc = total = None
        for t in range(T_LOCAL // TC):
            cols = slice(t * TC, (t + 1) * TC)
            if b < NB:
                s = dot_t(q, kb[b, cols])
                sbuf[b % 2, :, cols] = s
                for z in range(TC // 128):
                    piece = s[:, 128 * z : 128 * z + 128]
                    peak = piece if peak is None else jnp.maximum(peak, piece)
            if b > 0:
                w = jnp.exp2(sbuf[(b - 1) % 2, :, cols] * SCALE2 - prev_peak)
                for z in range(TC // 128):
                    piece = w[:, 128 * z : 128 * z + 128]
                    total = piece if total is None else total + piece
                o = dot(w.astype(BF), vb[b - 1, cols])
                acc = o if acc is None else acc + o
        if b > 0:
            finish(b - 1, acc, prev_top, total.sum(1, keepdims=True))
        if b < NB:
            prev_top = peak.max(1, keepdims=True)
            prev_peak = prev_top * SCALE2
    for send in sends:
        send.wait()


def prefix_call(prompt, q, tail, keys, values):
    return pl.pallas_call(
        prefix_kernel,
        out_shape=jax.ShapeDtypeStruct((DEST, ROWS, 128), BF),
        in_specs=[VMEM, VMEM, ANY, ANY, ANY],
        out_specs=ANY,
        scratch_shapes=[
            pltpu.VMEM((NB, 256, 128), BF),
            pltpu.VMEM((NB, T_LOCAL, HD), BF),
            pltpu.VMEM((NB, T_LOCAL, HD), BF),
            pltpu.VMEM((2, 256, T_LOCAL), F32),
            pltpu.VMEM((2, KVH, 4, 128), F32),
            pltpu.VMEM((DEST, 32, 128), F32),
            pltpu.VMEM((DEST, ROWS, 128), BF),
            pltpu.VMEM((64, HEADS * HD), F32),
            pltpu.VMEM((64, HEADS * HD), BF),
            pltpu.SemaphoreType.DMA,
            pltpu.SemaphoreType.DMA((NB,)),
            pltpu.SemaphoreType.DMA((NB,)),
            pltpu.SemaphoreType.DMA((KVH,)),
        ],
        compiler_params=pltpu.CompilerParams(vmem_limit_bytes=50 * 2**20),
        cost_estimate=pl.CostEstimate(flops=9 * 10**9, bytes_accessed=18 * 2**20, transcendentals=2**23),
        name="prefix",
    )(prompt, q, tail, keys, values)


def pack_kernel(*refs):
    w_hbm, out_ref, sem = refs[:8], refs[8], refs[9]
    loads = [pltpu.make_async_copy(w_hbm[n], out_ref.at[n], sem.at[n]) for n in range(8)]
    for load in loads:
        load.start()
    for load in loads:
        load.wait()


def pack_call(weights):
    return pl.pallas_call(
        pack_kernel,
        out_shape=jax.ShapeDtypeStruct((8, 512, 512), BF),
        in_specs=[ANY] * 8,
        out_specs=ANY,
        scratch_shapes=[pltpu.SemaphoreType.DMA((8,))],
        compiler_params=pltpu.CompilerParams(vmem_limit_bytes=16 * 2**20),
        cost_estimate=pl.CostEstimate(flops=0, bytes_accessed=8 * 2**20, transcendentals=0),
        name="pack",
    )(*weights)


def project_kernel(r_ref, pm_ref, un_ref, w_hbm, z_ref, wv, yv, zf, wsem):
    loads = [pltpu.make_async_copy(w_hbm.at[n], wv.at[n], wsem.at[n]) for n in range(8)]
    for load in loads[:4]:
        load.start()
    f = lambda x: x.astype(F32)
    lane = iota((256, 128), 1)
    row = iota((256, 128), 0)
    pad = jnp.zeros((112, 128), F32)
    logs = []
    for half in range(2):
        part = f(r_ref[:, 272 + half]) + f(r_ref[:, 274 + half]) + f(r_ref[:, 276 + half])
        logs.append(jnp.transpose(jnp.concatenate([part, pad], 0)))
    logs = jnp.concatenate(logs, 0)
    cont = r_ref[:, 256:272].reshape(256, 128)
    terms = jnp.zeros((256, 128), F32)
    for n in range(3):
        term = jnp.broadcast_to(f(r_ref[:, 278 + n])[:, None, :], (16, 16, 128)).reshape(256, 128)
        term = jnp.where(lane == (row & 15), term, 0.0).sum(1, keepdims=True)
        terms = terms + jnp.where(lane == n, jnp.broadcast_to(term, (256, 128)), 0.0)
    moved = dot(pm_ref[...], jnp.concatenate([cont, terms.astype(BF)], 1))
    for load in loads[:4]:
        load.wait()
    for load in loads[4:]:
        load.start()
    log_c = moved[:, 128:129] + moved[:, 129:130] + moved[:, 130:131]
    top = jnp.maximum(jnp.where(lane < 16, logs, -jnp.inf).max(1, keepdims=True), log_c)
    w_c = jnp.exp2(log_c - top)
    w_p = jnp.exp2(jnp.where(lane < 16, logs - top, -jnp.inf))
    den = w_p.sum(1, keepdims=True) + w_c
    num = w_c * moved[:, :128]
    for src in range(16):
        num = num + w_p[:, src : src + 1] * f(r_ref[src, :256])
    mixed = (num / den).astype(BF).reshape(4, 4, 16, 128)
    mixed = jnp.concatenate([mixed[:, jj].reshape(64, 128) for jj in range(4)], 1)
    mixed = dot(un_ref[...], mixed).astype(BF)
    member = lax.axis_index("group")
    z, core = member >> 1, member & 1
    for n in range(8):
        if n == 4:
            for load in loads[4:]:
                load.wait()
        g = 2 * ((z - n % 4) & 3) + (core if n < 4 else 1 - core)
        yv[g] = dot(mixed, wv[n])
    for g in range(8):
        cols = slice(512 * (g % 2), 512 * (g % 2) + 512)
        zf[:, 4 * (g // 2) : 4 * (g // 2) + 4, cols] = yv[g].reshape(DEST, 4, 512)
    z_ref[...] = zf[...].astype(BF)


def project_call(received, pm, unsort, weights):
    return pl.pallas_call(
        project_kernel,
        out_shape=jax.ShapeDtypeStruct((DEST, 16, 1024), BF),
        in_specs=[VMEM] * 3 + [ANY],
        out_specs=VMEM,
        scratch_shapes=[
            pltpu.VMEM((8, 512, 512), BF),
            pltpu.VMEM((8, 64, 512), F32),
            pltpu.VMEM((DEST, 16, 1024), F32),
            pltpu.SemaphoreType.DMA((8,)),
        ],
        compiler_params=pltpu.CompilerParams(vmem_limit_bytes=52 * 2**20),
        cost_estimate=pl.CostEstimate(flops=3 * 10**8, bytes_accessed=4 * 2**20, transcendentals=2**15),
        name="project",
    )(received, pm, unsort, weights)


def sum_kernel(r_ref, o_ref):
    total = r_ref[0].astype(F32)
    for src in range(1, DEST):
        total = total + r_ref[src].astype(F32)
    for quarter in range(4):
        o_ref[0, :, 1024 * quarter : 1024 * quarter + 1024] = total[
            4 * quarter : 4 * quarter + 4
        ].astype(BF)


def sum_call(received):
    return pl.pallas_call(
        sum_kernel,
        out_shape=jax.ShapeDtypeStruct((1, 4, D), BF),
        in_specs=[VMEM],
        out_specs=VMEM,
        compiler_params=pltpu.CompilerParams(vmem_limit_bytes=16 * 2**20),
        name="sum",
    )(received)


def gather_weights(w_out, seq):
    own = lax.optimization_barrier(lax.dynamic_slice_in_dim(w_out, 4 * seq * HD, 4 * HD, 0))
    blocks = [own]
    for k in (1, 2, 3):
        hop = [(2 * a + c, 2 * ((a + k) % 4) + c) for a in range(4) for c in range(2)]
        blocks.append(lax.ppermute(own, "group", hop))
    return blocks


def per_device(
    queries, prefix_keys, prefix_values, cont_keys, cont_values, cont_len, prompt_of, w_out
):
    copies = copies_call(queries)
    copies, w_out = lax.optimization_barrier((copies, w_out))
    gathered = lax.all_to_all(copies, "seq", 0, 0)
    weights = gather_weights(w_out, lax.axis_index("seq"))
    tail, pm, unsort = cont_call(cont_len[0], prompt_of, queries, cont_keys[0], cont_values[0])
    part = prefix_call(prompt_of, gathered, tail, prefix_keys[0], prefix_values[0])
    part, weights = lax.optimization_barrier((part, weights))
    swap = [(j, j ^ 1) for j in range(8)]
    weights = weights + [lax.ppermute(b, "group", swap) for b in weights]
    received = lax.all_to_all(part, "seq", 0, 0)
    y = project_call(received, pm, unsort, pack_call(weights))
    return sum_call(lax.all_to_all(y, "seq", 0, 0))


def solution(mesh):
    return jax.shard_map(
        per_device,
        mesh=mesh,
        in_specs=(
            P("group", "seq", None),
            P("group", None, None, "seq", None),
            P("group", None, None, "seq", None),
            P("group", "seq", None, None, None),
            P("group", "seq", None, None, None),
            P("group", "seq"),
            P("group", None),
            P(None, "group"),
        ),
        out_specs=P("group", "seq", None),
        check_vma=False,
    )
```
